32 devices in a mesh: grp: 2 (over x), hid: 16 (over z, y, core).
Axes of the slice: x: 2, y: 2, z: 4, core: 2. Of those that a mesh axis runs over, the one named last changes fastest.
Arguments:
- tokens: bfloat16 [64, 8192], P(('grp', 'hid')), parts along dimension 0, may hold values from -6 to 6
- gate_blocks: bfloat16 [64, 48, 128, 128], P(('grp', 'hid')), parts along dimension 0, may hold values from -0.09375 to 0.09375
- up_blocks: bfloat16 [64, 48, 128, 128], P(('grp', 'hid')), parts along dimension 0, may hold values from -0.09375 to 0.09375
- down_blocks: bfloat16 [64, 48, 128, 128], P(('grp', 'hid')), parts along dimension 0, may hold values from -0.1875 to 0.1875
- block_index: int32 [64, 3, 48], P(('grp', 'hid')), parts along dimension 0, may hold values from 0 to 63, as said below
- block_count: int32 [64, 3], P(('grp', 'hid')), parts along dimension 0, may hold values from 16 to 48, as said below
Outputs:
- mixed: bfloat16 [64, 8192], P(('grp', 'hid')), parts along dimension 0
The draws below stay inside these ranges and needn't reach their ends.
There are 2 independent parts, one for each index of `grp`. The reference program is written for one: setup_inputs(seed, part) draws one part's arguments, and reference() takes and returns one part's arrays. A program takes and returns all parts, laid end to end along the dimension named above; each array names one. Nothing has to cross between parts.
Inputs may be any that keep to these rules, and one draw needn't show every extreme that they name: `block_index`: for each shard and matrix the 48 slots name distinct width blocks; only the first block_count entries are kept, the rest must be ignored. `block_count`: in every draw, for each of the three matrices, some shard keeps exactly 48 blocks and some exactly 16.
All inputs are finite; a program needn't handle non-finite values.
Results may differ from the reference program's by a relative error of at most 0.0051.
Values may be sent and summed in bfloat16 or wider, within the bound.
No kernel may reach another device: no remote copies, remote signals or barrier semaphores. Data moves between devices by JAX's collectives and lax.ppermute only.
A program may use at most 128 MiB of HBM per device.

```python
import jax
import jax.numpy as jnp
from jax import lax

D = 8192
BLK = 128
DBLK = 64
KMAX = 48
HID_SHARDS = 32
FF = 4096
TOKENS = 32


def draw_block_index(key, part):
    key = jax.random.fold_in(key, 11)
    subkeys = jax.random.split(key, HID_SHARDS * 3)
    orders = jax.vmap(lambda subkey: jax.random.permutation(subkey, DBLK)[:KMAX])(subkeys)
    return orders.reshape(HID_SHARDS, 3, KMAX).astype(jnp.int32)


def draw_block_count(key, part):
    key = jax.random.fold_in(key, 23)
    columns = []
    for matrix in range(3):
        count_key = jax.random.fold_in(key, 2 * matrix)
        place_key = jax.random.fold_in(key, 2 * matrix + 1)
        counts = jax.random.randint(count_key, (HID_SHARDS,), DBLK // 4, KMAX + 1)
        order = jax.random.permutation(place_key, HID_SHARDS)
        counts = counts.at[order[0]].set(KMAX).at[order[1]].set(DBLK // 4)
        columns.append(counts)
    return jnp.stack(columns, axis=1).astype(jnp.int32)


def level_of(own_key, shape, pieces, smallest, largest):
    loudness = 1.0
    for dim, blocks in pieces:
        heights = jax.random.uniform(jax.random.fold_in(jax.random.fold_in(own_key, 6), dim), (blocks,), jnp.float32, smallest / len(pieces), largest / len(pieces))
        loudness = loudness * jnp.repeat(jnp.exp(heights), shape[dim] // blocks).reshape((-1,) + (1,) * (len(shape) - 1 - dim))
    return loudness


def noise(own_key, shape, scale, reach, cuts=(), held_as=jnp.bfloat16):
    values = scale * jax.random.normal(own_key, shape, jnp.float32)
    if cuts:
        values = values * level_of(own_key, shape, cuts, -0.22, 0.18)
    return jnp.clip(values, -reach, reach).astype(held_as)


def setup_inputs(seed: int = 0, part: int = 0) -> dict:
    key_of = jax.random.split(jax.random.key(seed), 7)
    part_splits = jax.random.split(jax.random.fold_in(key_of[6], part), 7)
    tokens = noise(part_splits[0], (TOKENS, D), 1.0, 6.0, ((0, 16),))
    gate_blocks = noise(part_splits[1], (HID_SHARDS, KMAX, BLK, BLK), (2 * KMAX * BLK // 3) ** -0.5, 0.09375, ((0, 16),))
    up_blocks = noise(part_splits[2], (HID_SHARDS, KMAX, BLK, BLK), (2 * KMAX * BLK // 3) ** -0.5, 0.09375, ((0, 16),))
    down_blocks = noise(part_splits[3], (HID_SHARDS, KMAX, BLK, BLK), (FF // 4) ** -0.5, 0.1875, ((0, 16),))
    block_index = draw_block_index(jax.random.fold_in(jax.random.fold_in(key_of[6], part), 71), part)
    block_count = draw_block_count(jax.random.fold_in(jax.random.fold_in(key_of[6], part), 71), part)
    return {"tokens": tokens, "gate_blocks": gate_blocks, "up_blocks": up_blocks, "down_blocks": down_blocks, "block_index": block_index, "block_count": block_count}


def reference(tokens, gate_blocks, up_blocks, down_blocks, block_index, block_count):
    grouped = tokens.reshape(TOKENS, DBLK, BLK)
    slots = jnp.arange(KMAX, dtype=jnp.int32)

    def advance(totals, sliced):
        gate_local, up_local, down_local, index_local, count_local = sliced
        usable = (slots[None, :] < count_local[:, None]).astype(jnp.float32)
        picked_gate = jnp.take(grouped, index_local[0], axis=1).astype(jnp.float32) * usable[0][None, :, None]
        picked_up = jnp.take(grouped, index_local[1], axis=1).astype(jnp.float32) * usable[1][None, :, None]
        gate = jnp.einsum("tkc,kcj->tj", picked_gate, gate_local.astype(jnp.float32))
        upper = jnp.einsum("tkc,kcj->tj", picked_up, up_local.astype(jnp.float32))
        hidden = (jax.nn.silu(gate) * upper).astype(jnp.bfloat16)
        partial_value = jnp.einsum("tj,kjc->tkc", hidden.astype(jnp.float32), down_local.astype(jnp.float32))
        partial_value = partial_value * usable[2][None, :, None]
        totals = totals.at[:, index_local[2]].add(partial_value)
        return totals, None

    start_totals = jnp.zeros((TOKENS, DBLK, BLK), jnp.float32)
    totals, unused = lax.scan(advance, start_totals, (gate_blocks, up_blocks, down_blocks, block_index, block_count))
    return totals.reshape(TOKENS, D).astype(jnp.bfloat16)
```

```python
import functools

import jax
import jax.numpy as jnp
from jax import lax
from jax.experimental import pallas as pl
from jax.experimental.pallas import tpu as pltpu
from jax.sharding import PartitionSpec as P


def exchange_stages(size):
    bits = []
    bit = size // 2
    while bit > 1:
        bits.append(bit)
        bit //= 2
    stages = [(b + 1,) for b in bits[:-2]]
    tail = bits[-2:]
    if len(tail) == 2:
        stages.append((tail[1] + 1, tail[0] + 1, tail[0] + tail[1] + 1))
    else:
        stages.extend((b + 1,) for b in tail)
    stages.append((1,))
    return stages


def swap(value, size, offset):
    return lax.ppermute(value, "hid", [(i, i ^ offset) for i in range(size)])


def slot_table(index_local, count_local, blocks):
    kslots = index_local.shape[-1]
    slots = jnp.arange(kslots, dtype=jnp.int32)
    names = jnp.arange(blocks, dtype=jnp.int32)
    kept = slots < count_local[:, :, None]
    hit = (index_local[:, :, :, None] == names) & kept[:, :, :, None]
    return jnp.min(jnp.where(hit, slots[:, None], kslots), axis=2)


def feed_forward_kernel(
    table_ref, own_ref, peer_ref, gate_ref, up_ref, down_ref, keep_ref, send_ref
):
    columns, kslots, block, _ = gate_ref.shape
    rows, width = own_ref.shape
    blocks = width // block

    def pick(ref, shard, matrix, name):
        slot = table_ref[(shard * 3 + matrix) * blocks + name]
        value = ref[shard, jnp.minimum(slot, kslots - 1)]
        return jnp.where(slot < kslots, value, jnp.zeros_like(value))

    total = jnp.zeros((2 * rows, 2 * columns * block), jnp.float32)

    def up_step(step, total):
        start = pl.multiple_of(step * 2 * block, 2 * block)
        left = jnp.concatenate(
            [own_ref[:, pl.ds(start, 2 * block)], peer_ref[:, pl.ds(start, 2 * block)]], axis=0
        )
        right = jnp.concatenate(
            [
                jnp.concatenate(
                    [
                        pick(ref, shard, matrix, 2 * step + half)
                        for shard in range(columns)
                        for matrix, ref in ((0, gate_ref), (1, up_ref))
                    ],
                    axis=1,
                )
                for half in range(2)
            ],
            axis=0,
        )
        return total + jnp.dot(left, right, preferred_element_type=jnp.float32)

    total = lax.fori_loop(0, blocks // 2, up_step, total, unroll=4)
    hidden = []
    for shard in range(columns):
        gate = total[:, 2 * shard * block : (2 * shard + 1) * block]
        upper = total[:, (2 * shard + 1) * block : (2 * shard + 2) * block]
        hidden.append((gate / (1.0 + jnp.exp(-gate)) * upper).astype(jnp.bfloat16))
    hidden = jnp.concatenate(hidden, axis=1)

    def down_step(step, carry):
        right = jnp.concatenate(
            [
                jnp.concatenate(
                    [pick(down_ref, shard, 2, 2 * step + half) for half in range(2)], axis=1
                )
                for shard in range(columns)
            ],
            axis=0,
        )
        value = jnp.dot(hidden, right, preferred_element_type=jnp.float32)
        start = pl.multiple_of(step * 2 * block, 2 * block)
        keep_ref[:, pl.ds(start, 2 * block)] = value[:rows]
        send_ref[:, pl.ds(start, 2 * block)] = value[rows:].astype(jnp.bfloat16)
        return carry

    lax.fori_loop(0, blocks // 2, down_step, 0, unroll=4)


def feed_forward(table, own, peer, gate_blocks, up_blocks, down_blocks):
    vmem = pl.BlockSpec(memory_space=pltpu.VMEM)
    smem = pl.BlockSpec(memory_space=pltpu.SMEM)
    return pl.pallas_call(
        feed_forward_kernel,
        out_shape=(
            jax.ShapeDtypeStruct(own.shape, jnp.float32),
            jax.ShapeDtypeStruct(own.shape, jnp.bfloat16),
        ),
        in_specs=[smem] + [vmem] * 5,
        out_specs=(vmem, vmem),
        compiler_params=pltpu.CompilerParams(vmem_limit_bytes=32 * 1024 * 1024),
        name="feed_forward",
    )(table, own, peer, gate_blocks, up_blocks, down_blocks)


def per_device(size, tokens, gate_blocks, up_blocks, down_blocks, block_index, block_count):
    blocks = tokens.shape[1] // gate_blocks.shape[-1]
    stages = exchange_stages(size)
    table = slot_table(block_index, block_count, blocks).reshape(-1)

    held = tokens
    for offsets in stages[:-1]:
        held = jnp.concatenate([held] + [swap(held, size, k) for k in offsets], axis=0)
    peer = swap(held, size, 1)

    total, send = feed_forward(table, held, peer, gate_blocks, up_blocks, down_blocks)

    total = total + swap(send, size, 1).astype(jnp.float32)
    for offsets in stages[-2::-1]:
        rows = total.shape[0] // (len(offsets) + 1)
        arrived = [
            swap(total[(i + 1) * rows : (i + 2) * rows].astype(jnp.bfloat16), size, k)
            for i, k in enumerate(offsets)
        ]
        total = total[:rows]
        for value in arrived:
            total = total + value.astype(jnp.float32)
    return total.astype(jnp.bfloat16)


def solution(mesh):
    return jax.shard_map(
        functools.partial(per_device, mesh.shape["hid"]),
        mesh=mesh,
        in_specs=(
            P(("grp", "hid"), None),
            P(("grp", "hid"), None, None, None),
            P(("grp", "hid"), None, None, None),
            P(("grp", "hid"), None, None, None),
            P(("grp", "hid"), None, None),
            P(("grp", "hid"), None),
        ),
        out_specs=P(("grp", "hid"), None),
        check_vma=False,
    )
```

```python
import functools

import jax
import jax.numpy as jnp
from jax import lax
from jax.experimental import pallas as pl
from jax.experimental.pallas import tpu as pltpu
from jax.sharding import PartitionSpec as P


def exchange_stages(size):
    bits = []
    bit = size // 2
    while bit > 1:
        bits.append(bit)
        bit //= 2
    stages = [(b + 1,) for b in bits[:-2]]
    tail = bits[-2:]
    if len(tail) == 2:
        stages.append((tail[1] + 1, tail[0] + 1, tail[0] + tail[1] + 1))
    else:
        stages.extend((b + 1,) for b in tail)
    stages.append((1,))
    return stages


def swap(value, size, offset):
    return lax.ppermute(value, "hid", [(i, i ^ offset) for i in range(size)])


def place_rows(value, before, after):
    return lax.pad(value, jnp.zeros((), value.dtype), ((before, after, 0), (0, 0, 0)))


def stack_rows(own, arrived):
    rows = own.shape[0]
    many = len(arrived)
    total = lax.optimization_barrier(place_rows(own, 0, many * rows))
    for i, value in enumerate(arrived):
        total = total + place_rows(value, (i + 1) * rows, (many - 1 - i) * rows)
    return total


def invert_kernel(index_ref, count_ref, leaving_ref):
    columns = count_ref.shape[0]
    blocks = leaving_ref.shape[1]

    def clear(name, carry):
        for row in range(columns + 1):
            leaving_ref[row, name] = 0
        return carry

    lax.fori_loop(0, blocks, clear, 0, unroll=8)
    for shard in range(columns):

        def enter(slot, carry):
            name = index_ref[2, shard, slot]
            leaving_ref[shard, name] = slot
            leaving_ref[columns, name] = leaving_ref[columns, name] + (1 << shard)
            return carry

        lax.fori_loop(0, count_ref[shard, 2], enter, 0)


def invert_lists(index, count, blocks):
    smem = pl.BlockSpec(memory_space=pltpu.SMEM)
    return pl.pallas_call(
        invert_kernel,
        out_shape=jax.ShapeDtypeStruct((count.shape[0] + 1, blocks), jnp.int32),
        in_specs=[smem, smem],
        out_specs=smem,
        compiler_params=pltpu.CompilerParams(vmem_limit_bytes=1024 * 1024),
        cost_estimate=pl.CostEstimate(flops=10000000000, bytes_accessed=1000, transcendentals=0),
        name="invert_lists",
    )(index, count)


def feed_forward_kernel(
    index_ref,
    count_ref,
    leaving_ref,
    own_ref,
    peer_ref,
    gate_ref,
    up_ref,
    down_ref,
    keep_ref,
    send_ref,
    token_ref,
    hidden_ref,
):
    columns, kslots, block, _ = gate_ref.shape
    rows, width = own_ref.shape
    blocks = width // block

    for name in range(blocks):
        lanes = slice(name * block, (name + 1) * block)
        token_ref[name, :rows] = own_ref[:, lanes]
        token_ref[name, rows:] = peer_ref[:, lanes]
    token_ref[blocks] = jnp.zeros(token_ref.shape[1:], token_ref.dtype)

    hidden = []
    for shard in range(columns):
        parts = []
        for matrix, ref in enumerate((gate_ref, up_ref)):
            count = count_ref[shard, matrix]
            total = jnp.zeros((2 * rows, block), jnp.float32)
            for slot in range(0, kslots, 2):
                names = [
                    jnp.where(slot + i < count, index_ref[matrix, shard, slot + i], blocks)
                    for i in range(2)
                ]
                left = jnp.concatenate([token_ref[name] for name in names], axis=1)
                right = ref[shard, slot : slot + 2].reshape(2 * block, block)
                total = total + jnp.dot(left, right, preferred_element_type=jnp.float32)
            parts.append(total)
        gate, upper = parts
        hidden.append((gate / (1.0 + jnp.exp(-gate)) * upper).astype(jnp.bfloat16))
    for mask in range(2**columns):
        hidden_ref[mask] = jnp.concatenate(
            [h if mask >> shard & 1 else jnp.zeros_like(h) for shard, h in enumerate(hidden)],
            axis=1,
        )

    for name in range(blocks):
        left = hidden_ref[leaving_ref[columns, name]]
        right = jnp.concatenate(
            [down_ref[shard, leaving_ref[shard, name]] for shard in range(columns)], axis=0
        )
        value = jnp.dot(left, right, preferred_element_type=jnp.float32)
        lanes = slice(name * block, (name + 1) * block)
        keep_ref[:, lanes] = value[:rows]
        send_ref[:, lanes] = value[rows:].astype(jnp.bfloat16)


def feed_forward(index, count, leaving, own, peer, gate_blocks, up_blocks, down_blocks):
    columns, _, block, _ = gate_blocks.shape
    rows, width = own.shape
    vmem = pl.BlockSpec(memory_space=pltpu.VMEM)
    smem = pl.BlockSpec(memory_space=pltpu.SMEM)
    size = gate_blocks.size + up_blocks.size + down_blocks.size
    return pl.pallas_call(
        feed_forward_kernel,
        out_shape=(
            jax.ShapeDtypeStruct(own.shape, jnp.float32),
            jax.ShapeDtypeStruct(own.shape, jnp.bfloat16),
        ),
        in_specs=[smem] * 3 + [vmem] * 5,
        out_specs=(vmem, vmem),
        scratch_shapes=[
            pltpu.VMEM((width // block + 1, 2 * rows, block), own.dtype),
            pltpu.VMEM((2**columns, 2 * rows, columns * block), jnp.bfloat16),
        ],
        compiler_params=pltpu.CompilerParams(vmem_limit_bytes=16 * 1024 * 1024),
        cost_estimate=pl.CostEstimate(
            flops=4 * rows * size, bytes_accessed=2 * size, transcendentals=0
        ),
        name="feed_forward",
    )(index, count, leaving, own, peer, gate_blocks, up_blocks, down_blocks)


def per_device(size, tokens, gate_blocks, up_blocks, down_blocks, block_index, block_count):
    stages = exchange_stages(size)
    index = jnp.transpose(block_index, (1, 0, 2))

    blocks = tokens.shape[1] // gate_blocks.shape[-1]

    held = tokens
    for number, offsets in enumerate(stages[:-1]):
        arrived = [swap(held, size, k) for k in offsets]
        if number == len(stages) - 2:
            index, held = lax.optimization_barrier((index, held))
            leaving = invert_lists(index, block_count, blocks)
            leaving, *arrived = lax.optimization_barrier((leaving, *arrived))
        held = stack_rows(held, arrived)
    peer = swap(held, size, 1)

    total, send = feed_forward(
        index, block_count, leaving, held, peer, gate_blocks, up_blocks, down_blocks
    )

    total = total + swap(send, size, 1).astype(jnp.float32)
    for offsets in stages[-2::-1]:
        rows = total.shape[0] // (len(offsets) + 1)
        arrived = [
            swap(total[(i + 1) * rows : (i + 2) * rows].astype(jnp.bfloat16), size, k)
            for i, k in enumerate(offsets)
        ]
        total = total[:rows]
        for value in arrived:
            total = total + value.astype(jnp.float32)
    return total.astype(jnp.bfloat16)


def solution(mesh):
    return jax.shard_map(
        functools.partial(per_device, mesh.shape["hid"]),
        mesh=mesh,
        in_specs=(
            P(("grp", "hid"), None),
            P(("grp", "hid"), None, None, None),
            P(("grp", "hid"), None, None, None),
            P(("grp", "hid"), None, None, None),
            P(("grp", "hid"), None, None),
            P(("grp", "hid"), None),
        ),
        out_specs=P(("grp", "hid"), None),
        check_vma=False,
    )
```

```python
import functools

import jax
import jax.numpy as jnp
from jax import lax
from jax.experimental import pallas as pl
from jax.experimental.pallas import tpu as pltpu
from jax.sharding import PartitionSpec as P


def exchange_stages(size):
    bits = []
    bit = size // 2
    while bit > 1:
        bits.append(bit)
        bit //= 2
    stages = [(b + 1,) for b in bits[:-2]]
    tail = bits[-2:]
    if len(tail) == 2:
        stages.append((tail[1] + 1, tail[0] + 1, tail[0] + tail[1] + 1))
    else:
        stages.extend((b + 1,) for b in tail)
    stages.append((1,))
    return stages


def far_first(many):
    return [many, *range(1, many)]


def swap(value, size, offset):
    return lax.ppermute(value, "hid", [(i, i ^ offset) for i in range(size)])


def place_rows(value, before, after):
    return lax.pad(value, jnp.zeros((), value.dtype), ((before, after, 0), (0, 0, 0)))


def stack_rows(parts):
    rows = parts[0].shape[0]
    many = len(parts)
    total = place_rows(parts[0], 0, (many - 1) * rows)
    for i, value in enumerate(parts[1:], 1):
        total = total + place_rows(value, i * rows, (many - 1 - i) * rows)
    return total


def hold_kernel(token_ref, held_ref):
    held_ref[...] = token_ref[...]


def hold(tokens):
    vmem = pl.BlockSpec(memory_space=pltpu.VMEM)
    return pl.pallas_call(
        hold_kernel,
        out_shape=jax.ShapeDtypeStruct(tokens.shape, tokens.dtype),
        in_specs=[vmem],
        out_specs=vmem,
        compiler_params=pltpu.CompilerParams(vmem_limit_bytes=1024 * 1024),
        cost_estimate=pl.CostEstimate(flops=10**10, bytes_accessed=1000, transcendentals=0),
        name="hold_tokens",
    )(tokens)


def feed_forward_kernel(
    index_ref,
    count_ref,
    own_ref,
    peer_ref,
    gate_ref,
    up_ref,
    down_ref,
    keep_ref,
    send_ref,
    token_ref,
    hidden_ref,
    slot_ref,
):
    columns, kslots, block, _ = gate_ref.shape
    rows, width = own_ref.shape
    blocks = width // block

    for shard in range(columns):
        for name in range(blocks):
            slot_ref[shard, name] = -1
        count = count_ref[shard, 2]
        for slot in range(kslots):
            name = jnp.where(slot < count, index_ref[2, shard, slot], blocks)
            slot_ref[shard, name] = slot

    for name in range(blocks):
        lanes = slice(name * block, (name + 1) * block)
        token_ref[name, :rows] = own_ref[:, lanes]
        token_ref[name, rows:] = peer_ref[:, lanes]
    token_ref[blocks] = jnp.zeros(token_ref.shape[1:], token_ref.dtype)

    hidden = []
    for shard in range(columns):
        parts = []
        for matrix, ref in enumerate((gate_ref, up_ref)):
            count = count_ref[shard, matrix]
            total = jnp.zeros((2 * rows, block), jnp.float32)
            for slot in range(0, kslots, 2):
                names = [
                    jnp.where(slot + i < count, index_ref[matrix, shard, slot + i], blocks)
                    for i in range(2)
                ]
                left = jnp.concatenate([token_ref[name] for name in names], axis=1)
                right = ref[shard, slot : slot + 2].reshape(2 * block, block)
                total = total + jnp.dot(left, right, preferred_element_type=jnp.float32)
            parts.append(total)
        gate, upper = parts
        hidden.append((gate / (1.0 + jnp.exp(-gate)) * upper).astype(jnp.bfloat16))
    for mask in range(2**columns):
        hidden_ref[mask] = jnp.concatenate(
            [h if mask >> shard & 1 else jnp.zeros_like(h) for shard, h in enumerate(hidden)],
            axis=1,
        )

    for name in range(blocks):
        slots = [slot_ref[shard, name] for shard in range(columns)]
        mask = sum(jnp.where(slot >= 0, 1 << shard, 0) for shard, slot in enumerate(slots))
        left = hidden_ref[mask]
        right = jnp.concatenate(
            [down_ref[shard, jnp.maximum(slot, 0)] for shard, slot in enumerate(slots)], axis=0
        )
        value = jnp.dot(left, right, preferred_element_type=jnp.float32)
        lanes = slice(name * block, (name + 1) * block)
        keep_ref[:, lanes] = value[:rows]
        send_ref[:, lanes] = value[rows:].astype(jnp.bfloat16)


def feed_forward(index, count, own, peer, gate_blocks, up_blocks, down_blocks):
    columns, _, block, _ = gate_blocks.shape
    rows, width = own.shape
    vmem = pl.BlockSpec(memory_space=pltpu.VMEM)
    smem = pl.BlockSpec(memory_space=pltpu.SMEM)
    size = gate_blocks.size + up_blocks.size + down_blocks.size
    return pl.pallas_call(
        feed_forward_kernel,
        out_shape=(
            jax.ShapeDtypeStruct(own.shape, jnp.float32),
            jax.ShapeDtypeStruct(own.shape, jnp.bfloat16),
        ),
        in_specs=[smem] * 2 + [vmem] * 5,
        out_specs=(vmem, vmem),
        scratch_shapes=[
            pltpu.VMEM((width // block + 1, 2 * rows, block), own.dtype),
            pltpu.VMEM((2**columns, 2 * rows, columns * block), jnp.bfloat16),
            pltpu.SMEM((columns, width // block + 1), jnp.int32),
        ],
        compiler_params=pltpu.CompilerParams(vmem_limit_bytes=16 * 1024 * 1024),
        cost_estimate=pl.CostEstimate(
            flops=4 * rows * size, bytes_accessed=2 * size, transcendentals=0
        ),
        name="feed_forward",
    )(index, count, own, peer, gate_blocks, up_blocks, down_blocks)


def per_device(size, tokens, gate_blocks, up_blocks, down_blocks, block_index, block_count):
    stages = exchange_stages(size)
    index = jnp.transpose(block_index, (1, 0, 2))

    parts = [hold(tokens)] + [swap(tokens, size, k) for k in stages[0]]
    for offsets in stages[1:-1]:
        held = stack_rows(parts)
        parts = [held] + [swap(held, size, k) for k in offsets]
    own = stack_rows(parts)
    peer = stack_rows([swap(part, size, 1) for part in parts])

    total, send = feed_forward(
        index, block_count, own, peer, gate_blocks, up_blocks, down_blocks
    )

    total = total + swap(send, size, 1).astype(jnp.float32)
    for offsets in stages[-2::-1]:
        rows = total.shape[0] // (len(offsets) + 1)
        arrived = [
            swap(total[i * rows : (i + 1) * rows].astype(jnp.bfloat16), size, offsets[i - 1])
            for i in far_first(len(offsets))
        ]
        total = total[:rows]
        for value in arrived:
            total = total + value.astype(jnp.float32)
    return total.astype(jnp.bfloat16)


def solution(mesh):
    return jax.shard_map(
        functools.partial(per_device, mesh.shape["hid"]),
        mesh=mesh,
        in_specs=(
            P(("grp", "hid"), None),
            P(("grp", "hid"), None, None, None),
            P(("grp", "hid"), None, None, None),
            P(("grp", "hid"), None, None, None),
            P(("grp", "hid"), None, None),
            P(("grp", "hid"), None),
        ),
        out_specs=P(("grp", "hid"), None),
        check_vma=False,
    )
```

```python
import functools

import jax
import jax.numpy as jnp
from jax import lax
from jax.experimental import pallas as pl
from jax.experimental.pallas import tpu as pltpu
from jax.sharding import PartitionSpec as P


def exchange_stages(size):
    bits = []
    bit = size // 2
    while bit > 1:
        bits.append(bit)
        bit //= 2
    stages = [(b + 1,) for b in bits[:-2]]
    tail = bits[-2:]
    if len(tail) == 2:
        stages.append((tail[1] + 1, tail[0] + 1, tail[0] + tail[1] + 1))
    else:
        stages.extend((b + 1,) for b in tail)
    stages.append((1,))
    return stages


def far_first(many):
    return [many, *range(1, many)]


def swap(value, size, offset):
    return lax.ppermute(value, "hid", [(i, i ^ offset) for i in range(size)])


def place_rows(value, before, after):
    return lax.pad(value, jnp.zeros((), value.dtype), ((before, after, 0), (0, 0, 0)))


def stack_rows(parts):
    rows = parts[0].shape[0]
    many = len(parts)
    total = place_rows(parts[0], 0, (many - 1) * rows)
    for i, value in enumerate(parts[1:], 1):
        total = total + place_rows(value, i * rows, (many - 1 - i) * rows)
    return total


def hold_kernel(token_ref, held_ref):
    held_ref[...] = token_ref[...]


def hold(tokens):
    vmem = pl.BlockSpec(memory_space=pltpu.VMEM)
    return pl.pallas_call(
        hold_kernel,
        out_shape=jax.ShapeDtypeStruct(tokens.shape, tokens.dtype),
        in_specs=[vmem],
        out_specs=vmem,
        compiler_params=pltpu.CompilerParams(vmem_limit_bytes=1024 * 1024),
        cost_estimate=pl.CostEstimate(flops=10**10, bytes_accessed=1000, transcendentals=0),
        name="hold_tokens",
    )(tokens)


def list_kernel(index_ref, count_ref, entering_ref, leaving_ref):
    _, columns, kslots = entering_ref.shape
    blocks = leaving_ref.shape[1] - 1
    for shard in range(columns):
        for name in range(blocks):
            leaving_ref[shard, name] = -1
        for matrix in range(3):
            count = count_ref[shard, matrix]
            for slot in range(kslots):
                name = jnp.where(slot < count, index_ref[matrix, shard, slot], blocks)
                if matrix < 2:
                    entering_ref[matrix, shard, slot] = name
                else:
                    leaving_ref[shard, name] = slot


def list_tables(index, count, blocks):
    _, columns, kslots = index.shape
    smem = pl.BlockSpec(memory_space=pltpu.SMEM)
    return pl.pallas_call(
        list_kernel,
        out_shape=(
            pltpu.SMEM((2, columns, kslots), jnp.int32),
            pltpu.SMEM((columns, blocks + 1), jnp.int32),
        ),
        in_specs=[smem, smem],
        out_specs=(smem, smem),
        compiler_params=pltpu.CompilerParams(vmem_limit_bytes=1024 * 1024),
        name="list_tables",
    )(index, count)


def feed_forward_kernel(
    entering_ref,
    leaving_ref,
    own_ref,
    peer_ref,
    gate_ref,
    up_ref,
    down_ref,
    keep_ref,
    send_ref,
    token_ref,
    hidden_ref,
):
    columns, kslots, block, _ = gate_ref.shape
    rows, width = own_ref.shape
    blocks = width // block

    for name in range(blocks):
        lanes = slice(name * block, (name + 1) * block)
        token_ref[name, :rows] = own_ref[:, lanes]
        token_ref[name, rows:] = peer_ref[:, lanes]
    token_ref[blocks] = jnp.zeros(token_ref.shape[1:], token_ref.dtype)

    hidden = []
    for shard in range(columns):
        parts = []
        for matrix, ref in enumerate((gate_ref, up_ref)):
            total = jnp.zeros((2 * rows, block), jnp.float32)
            for slot in range(0, kslots, 2):
                left = jnp.concatenate(
                    [token_ref[entering_ref[matrix, shard, slot + i]] for i in range(2)], axis=1
                )
                right = ref[shard, slot : slot + 2].reshape(2 * block, block)
                total = total + jnp.dot(left, right, preferred_element_type=jnp.float32)
            parts.append(total)
        gate, upper = parts
        hidden.append((gate / (1.0 + jnp.exp(-gate)) * upper).astype(jnp.bfloat16))
    for mask in range(2**columns):
        hidden_ref[mask] = jnp.concatenate(
            [h if mask >> shard & 1 else jnp.zeros_like(h) for shard, h in enumerate(hidden)],
            axis=1,
        )

    for name in range(blocks):
        slots = [leaving_ref[shard, name] for shard in range(columns)]
        mask = sum(jnp.where(slot >= 0, 1 << shard, 0) for shard, slot in enumerate(slots))
        left = hidden_ref[mask]
        right = jnp.concatenate(
            [down_ref[shard, jnp.maximum(slot, 0)] for shard, slot in enumerate(slots)], axis=0
        )
        value = jnp.dot(left, right, preferred_element_type=jnp.float32)
        lanes = slice(name * block, (name + 1) * block)
        keep_ref[:, lanes] = value[:rows]
        send_ref[:, lanes] = value[rows:].astype(jnp.bfloat16)


def feed_forward(entering, leaving, own, peer, gate_blocks, up_blocks, down_blocks):
    columns, _, block, _ = gate_blocks.shape
    rows, width = own.shape
    vmem = pl.BlockSpec(memory_space=pltpu.VMEM)
    smem = pl.BlockSpec(memory_space=pltpu.SMEM)
    size = gate_blocks.size + up_blocks.size + down_blocks.size
    return pl.pallas_call(
        feed_forward_kernel,
        out_shape=(
            jax.ShapeDtypeStruct(own.shape, jnp.float32),
            jax.ShapeDtypeStruct(own.shape, jnp.bfloat16),
        ),
        in_specs=[smem] * 2 + [vmem] * 5,
        out_specs=(vmem, vmem),
        scratch_shapes=[
            pltpu.VMEM((width // block + 1, 2 * rows, block), own.dtype),
            pltpu.VMEM((2**columns, 2 * rows, columns * block), jnp.bfloat16),
        ],
        compiler_params=pltpu.CompilerParams(vmem_limit_bytes=16 * 1024 * 1024),
        cost_estimate=pl.CostEstimate(
            flops=4 * rows * size, bytes_accessed=2 * size, transcendentals=0
        ),
        name="feed_forward",
    )(entering, leaving, own, peer, gate_blocks, up_blocks, down_blocks)


def per_device(size, tokens, gate_blocks, up_blocks, down_blocks, block_index, block_count):
    stages = exchange_stages(size)
    blocks = tokens.shape[1] // gate_blocks.shape[-1]
    index = jnp.transpose(block_index, (1, 0, 2))

    parts = [hold(tokens)] + [swap(tokens, size, k) for k in stages[0]]
    for offsets in stages[1:-1]:
        held = stack_rows(parts)
        index, held = lax.optimization_barrier((index, held))
        parts = [held] + [swap(held, size, k) for k in offsets]
    entering, leaving = list_tables(index, block_count, blocks)
    entering, leaving, parts[-1] = lax.optimization_barrier((entering, leaving, parts[-1]))
    own = stack_rows(parts)
    peer = stack_rows([swap(part, size, 1) for part in parts])

    total, send = feed_forward(
        entering, leaving, own, peer, gate_blocks, up_blocks, down_blocks
    )

    total = total + swap(send, size, 1).astype(jnp.float32)
    for offsets in stages[-2::-1]:
        rows = total.shape[0] // (len(offsets) + 1)
        arrived = [
            swap(total[i * rows : (i + 1) * rows].astype(jnp.bfloat16), size, offsets[i - 1])
            for i in far_first(len(offsets))
        ]
        total = total[:rows]
        for value in arrived:
            total = total + value.astype(jnp.float32)
    return total.astype(jnp.bfloat16)


def solution(mesh):
    return jax.shard_map(
        functools.partial(per_device, mesh.shape["hid"]),
        mesh=mesh,
        in_specs=(
            P(("grp", "hid"), None),
            P(("grp", "hid"), None, None, None),
            P(("grp", "hid"), None, None, None),
            P(("grp", "hid"), None, None, None),
            P(("grp", "hid"), None, None),
            P(("grp", "hid"), None),
        ),
        out_specs=P(("grp", "hid"), None),
        check_vma=False,
    )
```

```python
import functools

import jax
import jax.numpy as jnp
from jax import lax
from jax.experimental import pallas as pl
from jax.experimental.pallas import tpu as pltpu
from jax.sharding import PartitionSpec as P


def exchange_stages(size):
    bits = []
    bit = size // 2
    while bit > 1:
        bits.append(bit)
        bit //= 2
    stages = [(b + 1,) for b in bits[:-2]]
    tail = bits[-2:]
    if len(tail) == 2:
        stages.append((tail[1] + 1, tail[0] + 1, tail[0] + tail[1] + 1))
    else:
        stages.extend((b + 1,) for b in tail)
    stages.append((1,))
    return stages


def far_first(many):
    return [many, *range(1, many)]


def swap(value, size, offset):
    return lax.ppermute(value, "hid", [(i, i ^ offset) for i in range(size)])


def place_rows(value, before, after, beside):
    return lax.pad(value, jnp.zeros((), value.dtype), ((before, after, 0), (0, beside, 0)))


def stack_rows(parts, beside=0):
    rows = parts[0].shape[0]
    many = len(parts)
    total = place_rows(parts[0], 0, (many - 1) * rows, beside)
    for i, value in enumerate(parts[1:], 1):
        total = total + place_rows(value, i * rows, (many - 1 - i) * rows, beside)
    return total


def hold_kernel(token_ref, held_ref):
    held_ref[...] = token_ref[...]


def hold(tokens):
    vmem = pl.BlockSpec(memory_space=pltpu.VMEM)
    return pl.pallas_call(
        hold_kernel,
        out_shape=jax.ShapeDtypeStruct(tokens.shape, tokens.dtype),
        in_specs=[vmem],
        out_specs=vmem,
        compiler_params=pltpu.CompilerParams(vmem_limit_bytes=1024 * 1024),
        cost_estimate=pl.CostEstimate(flops=4 * 10**10, bytes_accessed=1000, transcendentals=0),
        name="hold_tokens",
    )(tokens)


def own_lists_kernel(index_ref, count_ref, index_vmem, entering_ref, leaving_ref, inverse_ref):
    _, columns, kslots = entering_ref.shape
    blocks = inverse_ref.shape[1]

    names = lax.broadcasted_iota(jnp.int32, (blocks, kslots), 0)
    slots = lax.broadcasted_iota(jnp.int32, (blocks, kslots), 1)
    inverse = []
    for shard in range(columns):
        hit = (index_vmem[2, shard : shard + 1] == names) & (slots < count_ref[shard, 2])
        slot = jnp.where(hit, slots.astype(jnp.float32), -1.0)
        slot = jnp.broadcast_to(jnp.max(slot, axis=1, keepdims=True), (blocks, 128))
        inverse.append(jnp.transpose(slot)[:1])
    inverse_ref[...] = jnp.concatenate(inverse, axis=0).astype(jnp.int32)

    for shard in range(columns):
        for name in range(blocks):
            leaving_ref[shard, name] = -1
        for matrix in range(3):
            count = count_ref[shard, matrix]
            for slot in range(kslots):
                name = jnp.where(slot < count, index_ref[matrix, shard, slot], blocks)
                if matrix < 2:
                    entering_ref[matrix, shard, slot] = name
                else:
                    leaving_ref[shard, name] = slot


def own_lists(index, count, blocks):
    _, columns, kslots = index.shape
    smem = pl.BlockSpec(memory_space=pltpu.SMEM)
    vmem = pl.BlockSpec(memory_space=pltpu.VMEM)
    return pl.pallas_call(
        own_lists_kernel,
        out_shape=(
            pltpu.SMEM((2, columns, kslots), jnp.int32),
            pltpu.SMEM((columns, blocks + 1), jnp.int32),
            jax.ShapeDtypeStruct((columns, blocks), jnp.int32),
        ),
        in_specs=[smem, smem, vmem],
        out_specs=(smem, smem, vmem),
        compiler_params=pltpu.CompilerParams(vmem_limit_bytes=1024 * 1024),
        name="own_lists",
    )(index, count, index)


def peer_lists_kernel(inverse_ref, leaving_ref):
    for shard in range(inverse_ref.shape[0]):
        for name in range(inverse_ref.shape[1]):
            leaving_ref[shard, name] = inverse_ref[shard, name]


def peer_lists(inverse):
    smem = pl.BlockSpec(memory_space=pltpu.SMEM)
    return pl.pallas_call(
        peer_lists_kernel,
        out_shape=pltpu.SMEM(inverse.shape, jnp.int32),
        in_specs=[smem],
        out_specs=smem,
        compiler_params=pltpu.CompilerParams(vmem_limit_bytes=1024 * 1024),
        name="peer_lists",
    )(inverse)


def hidden_kernel(
    entering_ref, own_ref, peer_ref, gate_ref, up_ref, down_ref, masked_ref, send_ref
):
    columns, kslots, block, _ = gate_ref.shape
    rows = own_ref.shape[0]

    hidden = []
    for shard in range(columns):
        parts = []
        for matrix, blocks_ref in enumerate((gate_ref, up_ref)):
            total = jnp.zeros((2 * rows, block), jnp.float32)
            for slot in range(0, kslots, 2):
                lanes = [
                    pl.ds(pl.multiple_of(entering_ref[matrix, shard, slot + i] * block, block), block)
                    for i in range(2)
                ]
                left = jnp.concatenate(
                    [
                        jnp.concatenate([ref[:, lane] for lane in lanes], axis=1)
                        for ref in (own_ref, peer_ref)
                    ],
                    axis=0,
                )
                right = blocks_ref[shard, slot : slot + 2].reshape(2 * block, block)
                total = total + jnp.dot(left, right, preferred_element_type=jnp.float32)
            parts.append(total)
        gate, upper = parts
        hidden.append((gate / (1.0 + jnp.exp(-gate)) * upper).astype(jnp.bfloat16))
    send_ref[...] = jnp.concatenate([h[rows:] for h in hidden], axis=1)
    put_masked(jnp.concatenate([h[:rows] for h in hidden], axis=1), masked_ref)


def put_masked(hidden, masked_ref):
    many = masked_ref.shape[0]
    columns = many.bit_length() - 1
    block = hidden.shape[1] // columns
    parts = [hidden[:, shard * block : (shard + 1) * block] for shard in range(columns)]
    for mask in range(many):
        masked_ref[mask] = jnp.concatenate(
            [h if mask >> shard & 1 else jnp.zeros_like(h) for shard, h in enumerate(parts)],
            axis=1,
        )


def hidden_units(entering, own, peer, gate_blocks, up_blocks, down_blocks):
    columns, _, block, _ = gate_blocks.shape
    rows = own.shape[0]
    vmem = pl.BlockSpec(memory_space=pltpu.VMEM)
    smem = pl.BlockSpec(memory_space=pltpu.SMEM)
    size = gate_blocks.size + up_blocks.size
    return pl.pallas_call(
        hidden_kernel,
        out_shape=(
            jax.ShapeDtypeStruct((2**columns, rows, columns * block), jnp.bfloat16),
            jax.ShapeDtypeStruct((rows, columns * block), jnp.bfloat16),
        ),
        in_specs=[smem] + [vmem] * 5,
        out_specs=(vmem, vmem),
        compiler_params=pltpu.CompilerParams(vmem_limit_bytes=16 * 1024 * 1024),
        cost_estimate=pl.CostEstimate(
            flops=4 * rows * size, bytes_accessed=2 * size, transcendentals=0
        ),
        name="hidden_units",
    )(entering, own, peer, gate_blocks, up_blocks, down_blocks)


def down_term(leaving_ref, masked_ref, down_ref, name):
    columns = down_ref.shape[0]
    slots = [leaving_ref[shard, name] for shard in range(columns)]
    mask = sum(jnp.where(slot >= 0, 1 << shard, 0) for shard, slot in enumerate(slots))
    right = jnp.concatenate(
        [down_ref[shard, jnp.maximum(slot, 0)] for shard, slot in enumerate(slots)], axis=0
    )
    return jnp.dot(masked_ref[mask], right, preferred_element_type=jnp.float32)


def own_down_kernel(leaving_ref, masked_ref, down_ref, partial_ref):
    block = down_ref.shape[-1]
    for name in range(partial_ref.shape[1] // block):
        lanes = slice(name * block, (name + 1) * block)
        partial_ref[:, lanes] = down_term(leaving_ref, masked_ref, down_ref, name)


def peer_down_kernel(leaving_ref, hidden_ref, down_ref, partial_ref, keep_ref, send_ref, masked_ref):
    block = down_ref.shape[-1]
    rows = keep_ref.shape[0]
    put_masked(hidden_ref[...], masked_ref)
    for name in range(partial_ref.shape[1] // block):
        lanes = slice(name * block, (name + 1) * block)
        value = partial_ref[:, lanes] + down_term(leaving_ref, masked_ref, down_ref, name)
        keep_ref[:, lanes] = value[:rows]
        send_ref[:, lanes] = value.astype(jnp.bfloat16)


def own_down(leaving, masked, down_blocks, width):
    _, rows, _ = masked.shape
    vmem = pl.BlockSpec(memory_space=pltpu.VMEM)
    smem = pl.BlockSpec(memory_space=pltpu.SMEM)
    size = down_blocks.size
    return pl.pallas_call(
        own_down_kernel,
        out_shape=jax.ShapeDtypeStruct((rows, width), jnp.float32),
        in_specs=[smem] + [vmem] * 2,
        out_specs=vmem,
        compiler_params=pltpu.CompilerParams(vmem_limit_bytes=16 * 1024 * 1024),
        cost_estimate=pl.CostEstimate(
            flops=2 * rows * size, bytes_accessed=2 * size, transcendentals=0
        ),
        name="own_down",
    )(leaving, masked, down_blocks)


def peer_down(leaving, hidden, down_blocks, partial, kept_rows):
    rows, width = partial.shape
    columns = down_blocks.shape[0]
    vmem = pl.BlockSpec(memory_space=pltpu.VMEM)
    smem = pl.BlockSpec(memory_space=pltpu.SMEM)
    size = down_blocks.size
    return pl.pallas_call(
        peer_down_kernel,
        out_shape=(
            jax.ShapeDtypeStruct((kept_rows, width), jnp.float32),
            jax.ShapeDtypeStruct((rows, width), jnp.bfloat16),
        ),
        in_specs=[smem] + [vmem] * 3,
        out_specs=(vmem, vmem),
        scratch_shapes=[pltpu.VMEM((2**columns, *hidden.shape), jnp.bfloat16)],
        compiler_params=pltpu.CompilerParams(vmem_limit_bytes=16 * 1024 * 1024),
        cost_estimate=pl.CostEstimate(
            flops=2 * rows * size, bytes_accessed=2 * size, transcendentals=0
        ),
        name="peer_down",
    )(leaving, hidden, down_blocks, partial)


def per_device(size, tokens, gate_blocks, up_blocks, down_blocks, block_index, block_count):
    stages = exchange_stages(size)
    width = tokens.shape[1]
    blocks = width // gate_blocks.shape[-1]
    index = jnp.transpose(block_index, (1, 0, 2))

    parts = [hold(tokens)] + [swap(tokens, size, k) for k in stages[0]]
    peer_blocks = swap(down_blocks, size, 1)
    for offsets in stages[1:-1]:
        held = stack_rows(parts)
        index, held = lax.optimization_barrier((index, held))
        parts = [held] + [swap(held, size, k) for k in offsets]
    entering, leaving, inverse = own_lists(index, block_count, blocks)
    entering, leaving, inverse, peer_blocks, parts[-1] = lax.optimization_barrier(
        (entering, leaving, inverse, peer_blocks, parts[-1])
    )
    inverse, parts[1] = lax.optimization_barrier((swap(inverse, size, 1), parts[1]))
    block = gate_blocks.shape[-1]
    own = stack_rows(parts, block)
    peer = stack_rows([swap(part, size, 1) for part in parts], block)
    peer_leaving, peer = lax.optimization_barrier((peer_lists(inverse), peer))

    masked, hidden = hidden_units(
        entering, own, peer, gate_blocks, up_blocks, down_blocks
    )
    hidden = swap(hidden, size, 1)
    partial = own_down(leaving, masked, down_blocks, width)
    rows = own.shape[0] // len(parts)
    total, send = peer_down(peer_leaving, hidden, peer_blocks, partial, rows)
    leaving = {i: send[i * rows : (i + 1) * rows] for i in range(1, len(parts))}

    for offsets in stages[-2::-1]:
        many = len(offsets) + 1
        if not leaving:
            rows = total.shape[0] // many
            leaving = {
                i: total[i * rows : (i + 1) * rows].astype(jnp.bfloat16) for i in range(1, many)
            }
        arrived = [swap(leaving[i], size, offsets[i - 1]) for i in far_first(len(offsets))]
        total = total[:rows]
        for value in arrived:
            total = total + value.astype(jnp.float32)
        leaving = {}
    return total.astype(jnp.bfloat16)


def solution(mesh):
    return jax.shard_map(
        functools.partial(per_device, mesh.shape["hid"]),
        mesh=mesh,
        in_specs=(
            P(("grp", "hid"), None),
            P(("grp", "hid"), None, None, None),
            P(("grp", "hid"), None, None, None),
            P(("grp", "hid"), None, None, None),
            P(("grp", "hid"), None, None),
            P(("grp", "hid"), None),
        ),
        out_specs=P(("grp", "hid"), None),
        check_vma=False,
    )
```

```python
import functools

import jax
import jax.numpy as jnp
from jax import lax
from jax.experimental import pallas as pl
from jax.experimental.pallas import tpu as pltpu
from jax.sharding import PartitionSpec as P


def exchange_stages(size):
    bits = []
    bit = size // 2
    while bit > 1:
        bits.append(bit)
        bit //= 2
    stages = [(b + 1,) for b in bits[:-2]]
    tail = bits[-2:]
    if len(tail) == 2:
        stages.append((tail[1] + 1, tail[0] + 1, tail[0] + tail[1] + 1))
    else:
        stages.extend((b + 1,) for b in tail)
    stages.append((1,))
    return stages


def far_first(many):
    return [many, *range(1, many)]


def swap(value, size, offset):
    return lax.ppermute(value, "hid", [(i, i ^ offset) for i in range(size)])


def place_rows(value, before, after, beside):
    return lax.pad(value, jnp.zeros((), value.dtype), ((before, after, 0), (0, beside, 0)))


def stack_rows(parts, beside=0):
    rows = parts[0].shape[0]
    many = len(parts)
    total = place_rows(parts[0], 0, (many - 1) * rows, beside)
    for i, value in enumerate(parts[1:], 1):
        total = total + place_rows(value, i * rows, (many - 1 - i) * rows, beside)
    return total


def hold_kernel(token_ref, held_ref):
    held_ref[...] = token_ref[...]


def hold(tokens):
    vmem = pl.BlockSpec(memory_space=pltpu.VMEM)
    return pl.pallas_call(
        hold_kernel,
        out_shape=jax.ShapeDtypeStruct(tokens.shape, tokens.dtype),
        in_specs=[vmem],
        out_specs=vmem,
        compiler_params=pltpu.CompilerParams(vmem_limit_bytes=1024 * 1024),
        cost_estimate=pl.CostEstimate(flops=4 * 10**10, bytes_accessed=1000, transcendentals=0),
        name="hold_tokens",
    )(tokens)


def pace_kernel(out_ref):
    out_ref[...] = jnp.zeros_like(out_ref)


def pace(*arrays):
    mark = pl.pallas_call(
        pace_kernel,
        out_shape=jax.ShapeDtypeStruct((8, 128), jnp.float32),
        out_specs=pl.BlockSpec(memory_space=pltpu.VMEM),
        compiler_params=pltpu.CompilerParams(vmem_limit_bytes=1024 * 1024),
        cost_estimate=pl.CostEstimate(flops=4 * 10**10, bytes_accessed=1000, transcendentals=0),
        name="pace",
    )()
    return lax.optimization_barrier((*arrays, mark))[:-1]


def list_kernel(index_ref, count_ref, peer_index_ref, peer_count_ref, entering_ref, leaving_ref):
    _, _, columns, kslots = entering_ref.shape
    blocks = leaving_ref.shape[2] - 1
    for core, (names, counts) in enumerate(
        ((index_ref, count_ref), (peer_index_ref, peer_count_ref))
    ):
        for shard in range(columns):
            for name in range(blocks):
                leaving_ref[core, shard, name] = -1
            for matrix in range(3):
                count = counts[shard, matrix]
                for slot in range(kslots):
                    name = jnp.where(slot < count, names[matrix, shard, slot], blocks)
                    if matrix < 2:
                        entering_ref[core, matrix, shard, slot] = name
                    else:
                        leaving_ref[core, shard, name] = slot


def list_tables(index, count, peer_index, peer_count, blocks):
    _, columns, kslots = index.shape
    smem = pl.BlockSpec(memory_space=pltpu.SMEM)
    return pl.pallas_call(
        list_kernel,
        out_shape=(
            pltpu.SMEM((2, 2, columns, kslots), jnp.int32),
            pltpu.SMEM((2, columns, blocks + 1), jnp.int32),
        ),
        in_specs=[smem] * 4,
        out_specs=(smem, smem),
        compiler_params=pltpu.CompilerParams(vmem_limit_bytes=1024 * 1024),
        name="list_tables",
    )(index, count, peer_index, peer_count)


def hidden_kernel(
    entering_ref, token_ref, gate_ref, up_ref, peer_gate_ref, peer_up_ref, down_ref, masked_ref
):
    columns, kslots, block, _ = gate_ref.shape
    for core, pair in enumerate(((gate_ref, up_ref), (peer_gate_ref, peer_up_ref))):
        hidden = []
        for shard in range(columns):
            parts = []
            for matrix, ref in enumerate(pair):
                total = jnp.zeros((token_ref.shape[0], block), jnp.float32)
                for slot in range(0, kslots, 2):
                    starts = [entering_ref[core, matrix, shard, slot + i] * block for i in range(2)]
                    left = jnp.concatenate(
                        [token_ref[:, pl.ds(pl.multiple_of(start, block), block)] for start in starts],
                        axis=1,
                    )
                    right = ref[shard, slot : slot + 2].reshape(2 * block, block)
                    total = total + jnp.dot(left, right, preferred_element_type=jnp.float32)
                parts.append(total)
            gate, upper = parts
            hidden.append((gate / (1.0 + jnp.exp(-gate)) * upper).astype(jnp.bfloat16))
        for mask in range(2**columns):
            masked_ref[core, mask] = jnp.concatenate(
                [h if mask >> shard & 1 else jnp.zeros_like(h) for shard, h in enumerate(hidden)],
                axis=1,
            )


def hidden_units(entering, tokens, own, peer):
    gate_blocks, up_blocks, down_blocks = own
    columns, _, block, _ = gate_blocks.shape
    rows = tokens.shape[0]
    vmem = pl.BlockSpec(memory_space=pltpu.VMEM)
    smem = pl.BlockSpec(memory_space=pltpu.SMEM)
    size = 2 * (gate_blocks.size + up_blocks.size)
    return pl.pallas_call(
        hidden_kernel,
        out_shape=jax.ShapeDtypeStruct((2, 2**columns, rows, columns * block), jnp.bfloat16),
        in_specs=[smem] + [vmem] * 6,
        out_specs=vmem,
        compiler_params=pltpu.CompilerParams(vmem_limit_bytes=16 * 1024 * 1024),
        cost_estimate=pl.CostEstimate(
            flops=2 * rows * size, bytes_accessed=2 * size, transcendentals=0
        ),
        name="hidden_units",
    )(entering, tokens, gate_blocks, up_blocks, *peer, down_blocks)


def down_kernel(leaving_ref, masked_ref, down_ref, peer_down_ref, keep_ref, send_ref):
    columns, _, block, _ = down_ref.shape
    rows = keep_ref.shape[0]
    for name in range(send_ref.shape[1] // block):
        left, right = [], []
        for core, ref in enumerate((down_ref, peer_down_ref)):
            slots = [leaving_ref[core, shard, name] for shard in range(columns)]
            mask = sum(jnp.where(slot >= 0, 1 << shard, 0) for shard, slot in enumerate(slots))
            left.append(masked_ref[core, mask])
            right += [ref[shard, jnp.maximum(slot, 0)] for shard, slot in enumerate(slots)]
        value = jnp.dot(
            jnp.concatenate(left, axis=1),
            jnp.concatenate(right, axis=0),
            preferred_element_type=jnp.float32,
        )
        lanes = slice(name * block, (name + 1) * block)
        keep_ref[:, lanes] = value[:rows]
        send_ref[:, lanes] = value.astype(jnp.bfloat16)


def down_terms(leaving, masked, down_blocks, peer_blocks, width, kept_rows):
    rows = masked.shape[2]
    vmem = pl.BlockSpec(memory_space=pltpu.VMEM)
    smem = pl.BlockSpec(memory_space=pltpu.SMEM)
    size = 2 * down_blocks.size
    return pl.pallas_call(
        down_kernel,
        out_shape=(
            jax.ShapeDtypeStruct((kept_rows, width), jnp.float32),
            jax.ShapeDtypeStruct((rows, width), jnp.bfloat16),
        ),
        in_specs=[smem] + [vmem] * 3,
        out_specs=(vmem, vmem),
        compiler_params=pltpu.CompilerParams(vmem_limit_bytes=16 * 1024 * 1024),
        cost_estimate=pl.CostEstimate(
            flops=2 * rows * size, bytes_accessed=2 * size, transcendentals=0
        ),
        name="down_terms",
    )(leaving, masked, down_blocks, peer_blocks)


def per_device(size, tokens, gate_blocks, up_blocks, down_blocks, block_index, block_count):
    stages = exchange_stages(size)
    width = tokens.shape[1]
    block = gate_blocks.shape[-1]
    blocks = width // block
    index = jnp.transpose(block_index, (1, 0, 2))

    peer_index = swap(index, size, 1)
    peer_gate = swap(gate_blocks, size, 1)
    tokens, up_late = pace(tokens, up_blocks)
    own, count_late = lax.optimization_barrier((hold(tokens), block_count))
    parts = [own] + [swap(tokens, size, k) for k in stages[0]]
    peer_count = swap(count_late, size, 1)
    peer_up = swap(up_late, size, 1)
    for offsets in stages[1:-1]:
        held = stack_rows(parts)
        index, held = lax.optimization_barrier((index, held))
        parts = [held] + [swap(held, size, k) for k in offsets]
    peer_gate, peer_index, peer_count, down_late, index = lax.optimization_barrier(
        (peer_gate, peer_index, peer_count, down_blocks, index)
    )
    peer_down = swap(down_late, size, 1)
    entering, leaving = list_tables(index, block_count, peer_index, peer_count, blocks)
    entering, leaving, parts[-1] = lax.optimization_barrier((entering, leaving, parts[-1]))
    own = stack_rows(parts, block)

    masked = hidden_units(
        entering, own, (gate_blocks, up_blocks, down_blocks), (peer_gate, peer_up)
    )
    rows = own.shape[0] // len(parts)
    total, send = down_terms(leaving, masked, down_blocks, peer_down, width, rows)
    leaving = {i: send[i * rows : (i + 1) * rows] for i in range(1, len(parts))}

    for offsets in stages[-2::-1]:
        many = len(offsets) + 1
        if not leaving:
            rows = total.shape[0] // many
            leaving = {
                i: total[i * rows : (i + 1) * rows].astype(jnp.bfloat16) for i in range(1, many)
            }
        arrived = [swap(leaving[i], size, offsets[i - 1]) for i in ((1, 2, 3) if len(offsets) == 3 else (1,))]
        total = total[:rows]
        for value in arrived:
            total = total + value.astype(jnp.float32)
        leaving = {}
    return total.astype(jnp.bfloat16)


def solution(mesh):
    return jax.shard_map(
        functools.partial(per_device, mesh.shape["hid"]),
        mesh=mesh,
        in_specs=(
            P(("grp", "hid"), None),
            P(("grp", "hid"), None, None, None),
            P(("grp", "hid"), None, None, None),
            P(("grp", "hid"), None, None, None),
            P(("grp", "hid"), None, None),
            P(("grp", "hid"), None),
        ),
        out_specs=P(("grp", "hid"), None),
        check_vma=False,
    )
```

```python
import functools

import jax
import jax.numpy as jnp
from jax import lax
from jax.experimental import pallas as pl
from jax.experimental.pallas import tpu as pltpu
from jax.sharding import PartitionSpec as P


def exchange_stages(size):
    bits = []
    bit = size // 2
    while bit > 1:
        bits.append(bit)
        bit //= 2
    stages = [(b + 1,) for b in bits[:-2]]
    tail = bits[-2:]
    if len(tail) == 2:
        stages.append((tail[1] + 1, tail[0] + 1, tail[0] + tail[1] + 1))
    else:
        stages.extend((b + 1,) for b in tail)
    stages.append((1,))
    return stages


def far_first(many):
    return [many, *range(1, many)]


def swap(value, size, offset):
    return lax.ppermute(value, "hid", [(i, i ^ offset) for i in range(size)])


def place_rows(value, before, after, beside):
    return lax.pad(value, jnp.zeros((), value.dtype), ((before, after, 0), (0, beside, 0)))


def stack_rows(parts, beside=0):
    rows = parts[0].shape[0]
    many = len(parts)
    total = place_rows(parts[0], 0, (many - 1) * rows, beside)
    for i, value in enumerate(parts[1:], 1):
        total = total + place_rows(value, i * rows, (many - 1 - i) * rows, beside)
    return total


def hold_kernel(token_ref, held_ref):
    held_ref[...] = token_ref[...]


def hold(tokens):
    vmem = pl.BlockSpec(memory_space=pltpu.VMEM)
    return pl.pallas_call(
        hold_kernel,
        out_shape=jax.ShapeDtypeStruct(tokens.shape, tokens.dtype),
        in_specs=[vmem],
        out_specs=vmem,
        compiler_params=pltpu.CompilerParams(vmem_limit_bytes=1024 * 1024),
        cost_estimate=pl.CostEstimate(flops=4 * 10**10, bytes_accessed=1000, transcendentals=0),
        name="hold_tokens",
    )(tokens)


def pace_kernel(out_ref):
    out_ref[...] = jnp.zeros_like(out_ref)


def pace(*arrays):
    mark = pl.pallas_call(
        pace_kernel,
        out_shape=jax.ShapeDtypeStruct((8, 128), jnp.float32),
        out_specs=pl.BlockSpec(memory_space=pltpu.VMEM),
        compiler_params=pltpu.CompilerParams(vmem_limit_bytes=1024 * 1024),
        cost_estimate=pl.CostEstimate(flops=4 * 10**10, bytes_accessed=1000, transcendentals=0),
        name="pace",
    )()
    return lax.optimization_barrier((*arrays, mark))[:-1]


def list_kernel(index_ref, count_ref, peer_index_ref, peer_count_ref, entering_ref, leaving_ref):
    _, _, columns, kslots = entering_ref.shape
    blocks = leaving_ref.shape[2] - 1
    for core, (names, counts) in enumerate(
        ((index_ref, count_ref), (peer_index_ref, peer_count_ref))
    ):
        for shard in range(columns):
            for name in range(blocks):
                leaving_ref[core, shard, name] = -1
            for matrix in range(3):
                count = counts[shard, matrix]
                for slot in range(kslots):
                    name = jnp.where(slot < count, names[matrix, shard, slot], blocks)
                    if matrix < 2:
                        entering_ref[core, matrix, shard, slot] = name
                    else:
                        leaving_ref[core, shard, name] = slot


def list_tables(index, count, peer_index, peer_count, blocks):
    _, columns, kslots = index.shape
    smem = pl.BlockSpec(memory_space=pltpu.SMEM)
    return pl.pallas_call(
        list_kernel,
        out_shape=(
            pltpu.SMEM((2, 2, columns, kslots), jnp.int32),
            pltpu.SMEM((2, columns, blocks + 1), jnp.int32),
        ),
        in_specs=[smem] * 4,
        out_specs=(smem, smem),
        compiler_params=pltpu.CompilerParams(vmem_limit_bytes=1024 * 1024),
        name="list_tables",
    )(index, count, peer_index, peer_count)


def hidden_kernel(
    entering_ref, token_ref, gate_ref, up_ref, peer_gate_ref, peer_up_ref, down_ref, masked_ref
):
    columns, kslots, block, _ = gate_ref.shape
    for core, pair in enumerate(((gate_ref, up_ref), (peer_gate_ref, peer_up_ref))):
        hidden = []
        for shard in range(columns):
            parts = []
            for matrix, ref in enumerate(pair):
                total = jnp.zeros((token_ref.shape[0], block), jnp.float32)
                for slot in range(0, kslots, 2):
                    starts = [entering_ref[core, matrix, shard, slot + i] * block for i in range(2)]
                    left = jnp.concatenate(
                        [token_ref[:, pl.ds(pl.multiple_of(start, block), block)] for start in starts],
                        axis=1,
                    )
                    right = ref[shard, slot : slot + 2].reshape(2 * block, block)
                    total = total + jnp.dot(left, right, preferred_element_type=jnp.float32)
                parts.append(total)
            gate, upper = parts
            hidden.append((gate / (1.0 + jnp.exp(-gate)) * upper).astype(jnp.bfloat16))
        for mask in range(2**columns):
            masked_ref[core, mask] = jnp.concatenate(
                [h if mask >> shard & 1 else jnp.zeros_like(h) for shard, h in enumerate(hidden)],
                axis=1,
            )


def hidden_units(entering, tokens, own, peer):
    gate_blocks, up_blocks, down_blocks = own
    columns, _, block, _ = gate_blocks.shape
    rows = tokens.shape[0]
    vmem = pl.BlockSpec(memory_space=pltpu.VMEM)
    smem = pl.BlockSpec(memory_space=pltpu.SMEM)
    size = 2 * (gate_blocks.size + up_blocks.size)
    return pl.pallas_call(
        hidden_kernel,
        out_shape=jax.ShapeDtypeStruct((2, 2**columns, rows, columns * block), jnp.bfloat16),
        in_specs=[smem] + [vmem] * 6,
        out_specs=vmem,
        compiler_params=pltpu.CompilerParams(vmem_limit_bytes=16 * 1024 * 1024),
        cost_estimate=pl.CostEstimate(
            flops=2 * rows * size, bytes_accessed=2 * size, transcendentals=0
        ),
        name="hidden_units",
    )(entering, tokens, gate_blocks, up_blocks, *peer, down_blocks)


def down_kernel(leaving_ref, masked_ref, down_ref, peer_down_ref, keep_ref, *send_refs):
    columns, _, block, _ = down_ref.shape
    rows = keep_ref.shape[0]
    for name in range(keep_ref.shape[1] // block):
        left, right = [], []
        for core, ref in enumerate((down_ref, peer_down_ref)):
            slots = [leaving_ref[core, shard, name] for shard in range(columns)]
            mask = sum(jnp.where(slot >= 0, 1 << shard, 0) for shard, slot in enumerate(slots))
            left.append(masked_ref[core, mask])
            right += [ref[shard, jnp.maximum(slot, 0)] for shard, slot in enumerate(slots)]
        value = jnp.dot(
            jnp.concatenate(left, axis=1),
            jnp.concatenate(right, axis=0),
            preferred_element_type=jnp.float32,
        )
        lanes = slice(name * block, (name + 1) * block)
        keep_ref[:, lanes] = value[:rows]
        for i, send_ref in enumerate(send_refs, 1):
            send_ref[:, lanes] = value[i * rows : (i + 1) * rows].astype(jnp.bfloat16)


def down_terms(leaving, masked, down_blocks, peer_blocks, width, kept_rows):
    rows = masked.shape[2]
    vmem = pl.BlockSpec(memory_space=pltpu.VMEM)
    smem = pl.BlockSpec(memory_space=pltpu.SMEM)
    size = 2 * down_blocks.size
    return pl.pallas_call(
        down_kernel,
        out_shape=(
            jax.ShapeDtypeStruct((kept_rows, width), jnp.float32),
            *[jax.ShapeDtypeStruct((kept_rows, width), jnp.bfloat16)] * (rows // kept_rows - 1),
        ),
        in_specs=[smem] + [vmem] * 3,
        out_specs=(vmem,) * (rows // kept_rows),
        compiler_params=pltpu.CompilerParams(vmem_limit_bytes=16 * 1024 * 1024),
        cost_estimate=pl.CostEstimate(
            flops=2 * rows * size, bytes_accessed=2 * size, transcendentals=0
        ),
        name="down_terms",
    )(leaving, masked, down_blocks, peer_blocks)


def per_device(size, tokens, gate_blocks, up_blocks, down_blocks, block_index, block_count):
    stages = exchange_stages(size)
    width = tokens.shape[1]
    block = gate_blocks.shape[-1]
    blocks = width // block
    index = jnp.transpose(block_index, (1, 0, 2))

    peer_index = swap(index, size, 1)
    peer_gate = swap(gate_blocks, size, 1)
    tokens, up_late = pace(tokens, up_blocks)
    own, count_late = lax.optimization_barrier((hold(tokens), block_count))
    parts = [own] + [swap(tokens, size, k) for k in stages[0]]
    peer_count = swap(count_late, size, 1)
    peer_up = swap(up_late, size, 1)
    for offsets in stages[1:-1]:
        held = stack_rows(parts)
        index, held = lax.optimization_barrier((index, held))
        parts = [held] + [swap(held, size, k) for k in offsets]
    peer_gate, peer_index, peer_count, down_late, index = lax.optimization_barrier(
        (peer_gate, peer_index, peer_count, down_blocks, index)
    )
    peer_down = swap(down_late, size, 1)
    entering, leaving = list_tables(index, block_count, peer_index, peer_count, blocks)
    entering, leaving, parts[-1] = lax.optimization_barrier((entering, leaving, parts[-1]))
    own = stack_rows(parts, block)

    masked = hidden_units(
        entering, own, (gate_blocks, up_blocks, down_blocks), (peer_gate, peer_up)
    )
    rows = own.shape[0] // len(parts)
    total, *send = down_terms(leaving, masked, down_blocks, peer_down, width, rows)
    leaving = dict(enumerate(send, 1))

    for offsets in stages[-2::-1]:
        many = len(offsets) + 1
        if not leaving:
            rows = total.shape[0] // many
            leaving = {
                i: total[i * rows : (i + 1) * rows].astype(jnp.bfloat16) for i in range(1, many)
            }
        arrived = [swap(leaving[i], size, offsets[i - 1]) for i in ((1, 2, 3) if len(offsets) == 3 else (1,))]
        total = total[:rows]
        for value in arrived:
            total = total + value.astype(jnp.float32)
        leaving = {}
    return total.astype(jnp.bfloat16)


def solution(mesh):
    return jax.shard_map(
        functools.partial(per_device, mesh.shape["hid"]),
        mesh=mesh,
        in_specs=(
            P(("grp", "hid"), None),
            P(("grp", "hid"), None, None, None),
            P(("grp", "hid"), None, None, None),
            P(("grp", "hid"), None, None, None),
            P(("grp", "hid"), None, None),
            P(("grp", "hid"), None),
        ),
        out_specs=P(("grp", "hid"), None),
        check_vma=False,
    )
```

```python
import functools

import jax
import jax.numpy as jnp
from jax import lax
from jax.experimental import pallas as pl
from jax.experimental.pallas import tpu as pltpu
from jax.sharding import PartitionSpec as P


def exchange_stages(size):
    bits = []
    bit = size // 2
    while bit > 1:
        bits.append(bit)
        bit //= 2
    stages = [(b + 1,) for b in bits[:-2]]
    tail = bits[-2:]
    if len(tail) == 2:
        stages.append((tail[1] + 1, tail[0] + 1, tail[0] + tail[1] + 1))
    else:
        stages.extend((b + 1,) for b in tail)
    stages.append((1,))
    return stages


def far_first(many):
    return [many, *range(1, many)]


def swap(value, size, offset):
    return lax.ppermute(value, "hid", [(i, i ^ offset) for i in range(size)])


def place_rows(value, before, after, beside):
    return lax.pad(value, jnp.zeros((), value.dtype), ((before, after, 0), (0, beside, 0)))


def stack_rows(parts, beside=0):
    rows = parts[0].shape[0]
    many = len(parts)
    total = place_rows(parts[0], 0, (many - 1) * rows, beside)
    for i, value in enumerate(parts[1:], 1):
        total = total + place_rows(value, i * rows, (many - 1 - i) * rows, beside)
    return total


def sum_rows(terms, start, rows):
    return sum(term[start : start + rows].astype(jnp.float32) for term in terms)


def hold_kernel(token_ref, held_ref):
    held_ref[...] = token_ref[...]


def hold(tokens):
    vmem = pl.BlockSpec(memory_space=pltpu.VMEM)
    return pl.pallas_call(
        hold_kernel,
        out_shape=jax.ShapeDtypeStruct(tokens.shape, tokens.dtype),
        in_specs=[vmem],
        out_specs=vmem,
        compiler_params=pltpu.CompilerParams(vmem_limit_bytes=1024 * 1024),
        cost_estimate=pl.CostEstimate(flops=4 * 10**10, bytes_accessed=1000, transcendentals=0),
        name="hold_tokens",
    )(tokens)


def pace_kernel(out_ref):
    out_ref[...] = jnp.zeros_like(out_ref)


def pace(*arrays):
    mark = pl.pallas_call(
        pace_kernel,
        out_shape=jax.ShapeDtypeStruct((8, 128), jnp.float32),
        out_specs=pl.BlockSpec(memory_space=pltpu.VMEM),
        compiler_params=pltpu.CompilerParams(vmem_limit_bytes=1024 * 1024),
        cost_estimate=pl.CostEstimate(flops=4 * 10**10, bytes_accessed=1000, transcendentals=0),
        name="pace",
    )()
    return lax.optimization_barrier((*arrays, mark))[:-1]


def list_kernel(index_ref, count_ref, peer_index_ref, peer_count_ref, entering_ref, leaving_ref):
    _, _, columns, kslots = entering_ref.shape
    blocks = leaving_ref.shape[2] - 1
    for core, (names, counts) in enumerate(
        ((index_ref, count_ref), (peer_index_ref, peer_count_ref))
    ):
        for shard in range(columns):
            for name in range(blocks):
                leaving_ref[core, shard, name] = -1
            for matrix in range(3):
                count = counts[shard, matrix]
                for slot in range(kslots):
                    name = jnp.where(slot < count, names[matrix, shard, slot], blocks)
                    if matrix < 2:
                        entering_ref[core, matrix, shard, slot] = name
                    else:
                        leaving_ref[core, shard, name] = slot


def list_tables(index, count, peer_index, peer_count, blocks):
    _, columns, kslots = index.shape
    smem = pl.BlockSpec(memory_space=pltpu.SMEM)
    return pl.pallas_call(
        list_kernel,
        out_shape=(
            pltpu.SMEM((2, 2, columns, kslots), jnp.int32),
            pltpu.SMEM((2, columns, blocks + 1), jnp.int32),
        ),
        in_specs=[smem] * 4,
        out_specs=(smem, smem),
        compiler_params=pltpu.CompilerParams(vmem_limit_bytes=1024 * 1024),
        name="list_tables",
    )(index, count, peer_index, peer_count)


def hidden_kernel(
    entering_ref, token_ref, gate_ref, up_ref, peer_gate_ref, peer_up_ref, down_ref, masked_ref
):
    columns, kslots, block, _ = gate_ref.shape
    for core, pair in enumerate(((gate_ref, up_ref), (peer_gate_ref, peer_up_ref))):
        hidden = []
        for shard in range(columns):
            parts = []
            for matrix, ref in enumerate(pair):
                total = jnp.zeros((token_ref.shape[0], block), jnp.float32)
                for slot in range(0, kslots, 2):
                    starts = [entering_ref[core, matrix, shard, slot + i] * block for i in range(2)]
                    left = jnp.concatenate(
                        [token_ref[:, pl.ds(pl.multiple_of(start, block), block)] for start in starts],
                        axis=1,
                    )
                    right = ref[shard, slot : slot + 2].reshape(2 * block, block)
                    total = total + jnp.dot(left, right, preferred_element_type=jnp.float32)
                parts.append(total)
            gate, upper = parts
            hidden.append((gate / (1.0 + jnp.exp(-gate)) * upper).astype(jnp.bfloat16))
        for mask in range(2**columns):
            masked_ref[core, mask] = jnp.concatenate(
                [h if mask >> shard & 1 else jnp.zeros_like(h) for shard, h in enumerate(hidden)],
                axis=1,
            )


def hidden_units(entering, tokens, own, peer):
    gate_blocks, up_blocks, down_blocks = own
    columns, _, block, _ = gate_blocks.shape
    rows = tokens.shape[0]
    vmem = pl.BlockSpec(memory_space=pltpu.VMEM)
    smem = pl.BlockSpec(memory_space=pltpu.SMEM)
    size = 2 * (gate_blocks.size + up_blocks.size)
    return pl.pallas_call(
        hidden_kernel,
        out_shape=jax.ShapeDtypeStruct((2, 2**columns, rows, columns * block), jnp.bfloat16),
        in_specs=[smem] + [vmem] * 6,
        out_specs=vmem,
        compiler_params=pltpu.CompilerParams(vmem_limit_bytes=16 * 1024 * 1024),
        cost_estimate=pl.CostEstimate(
            flops=2 * rows * size, bytes_accessed=2 * size, transcendentals=0
        ),
        name="hidden_units",
    )(entering, tokens, gate_blocks, up_blocks, *peer, down_blocks)


def down_kernel(leaving_ref, masked_ref, down_ref, peer_down_ref, keep_ref, send_ref):
    columns, _, block, _ = down_ref.shape
    rows = keep_ref.shape[0]
    for name in range(send_ref.shape[1] // block):
        left, right = [], []
        for core, ref in enumerate((down_ref, peer_down_ref)):
            slots = [leaving_ref[core, shard, name] for shard in range(columns)]
            mask = sum(jnp.where(slot >= 0, 1 << shard, 0) for shard, slot in enumerate(slots))
            left.append(masked_ref[core, mask])
            right += [ref[shard, jnp.maximum(slot, 0)] for shard, slot in enumerate(slots)]
        value = jnp.dot(
            jnp.concatenate(left, axis=1),
            jnp.concatenate(right, axis=0),
            preferred_element_type=jnp.float32,
        )
        lanes = slice(name * block, (name + 1) * block)
        keep_ref[:, lanes] = value[:rows]
        send_ref[:, lanes] = value.astype(jnp.bfloat16)


def down_terms(leaving, masked, down_blocks, peer_blocks, width, kept_rows):
    rows = masked.shape[2]
    vmem = pl.BlockSpec(memory_space=pltpu.VMEM)
    smem = pl.BlockSpec(memory_space=pltpu.SMEM)
    size = 2 * down_blocks.size
    return pl.pallas_call(
        down_kernel,
        out_shape=(
            jax.ShapeDtypeStruct((kept_rows, width), jnp.float32),
            jax.ShapeDtypeStruct((rows, width), jnp.bfloat16),
        ),
        in_specs=[smem] + [vmem] * 3,
        out_specs=(vmem, vmem),
        compiler_params=pltpu.CompilerParams(vmem_limit_bytes=16 * 1024 * 1024),
        cost_estimate=pl.CostEstimate(
            flops=2 * rows * size, bytes_accessed=2 * size, transcendentals=0
        ),
        name="down_terms",
    )(leaving, masked, down_blocks, peer_blocks)


def per_device(size, tokens, gate_blocks, up_blocks, down_blocks, block_index, block_count):
    stages = exchange_stages(size)
    width = tokens.shape[1]
    block = gate_blocks.shape[-1]
    blocks = width // block
    index = jnp.transpose(block_index, (1, 0, 2))

    peer_index = swap(index, size, 1)
    peer_gate = swap(gate_blocks, size, 1)
    tokens, up_late = pace(tokens, up_blocks)
    own, count_late = lax.optimization_barrier((hold(tokens), block_count))
    parts = [own] + [swap(tokens, size, k) for k in stages[0]]
    peer_count = swap(count_late, size, 1)
    peer_up = swap(up_late, size, 1)
    for offsets in stages[1:-1]:
        held = stack_rows(parts)
        index, held = lax.optimization_barrier((index, held))
        parts = [held] + [swap(held, size, k) for k in offsets]
    peer_gate, peer_index, peer_count, down_late, index = lax.optimization_barrier(
        (peer_gate, peer_index, peer_count, down_blocks, index)
    )
    peer_down = swap(down_late, size, 1)
    entering, leaving = list_tables(index, block_count, peer_index, peer_count, blocks)
    entering, leaving, parts[-1] = lax.optimization_barrier((entering, leaving, parts[-1]))
    own = stack_rows(parts, block)

    masked = hidden_units(
        entering, own, (gate_blocks, up_blocks, down_blocks), (peer_gate, peer_up)
    )
    rows = own.shape[0] // len(parts)
    total, send = down_terms(leaving, masked, down_blocks, peer_down, width, rows)
    leaving = {i: send[i * rows : (i + 1) * rows] for i in range(1, len(parts))}

    terms = [total]
    for offsets in stages[-2::-1]:
        many = len(offsets) + 1
        if not leaving:
            rows = terms[0].shape[0] // many
            leaving = {
                i: sum_rows(terms, i * rows, rows).astype(jnp.bfloat16) for i in range(1, many)
            }
            leaving, terms = lax.optimization_barrier((leaving, terms))
            terms = [sum_rows(terms, 0, rows)]
        terms = terms + [swap(leaving[i], size, offsets[i - 1]) for i in range(1, many)]
        leaving = {}
    return sum_rows(terms, 0, rows).astype(jnp.bfloat16)


def solution(mesh):
    return jax.shard_map(
        functools.partial(per_device, mesh.shape["hid"]),
        mesh=mesh,
        in_specs=(
            P(("grp", "hid"), None),
            P(("grp", "hid"), None, None, None),
            P(("grp", "hid"), None, None, None),
            P(("grp", "hid"), None, None, None),
            P(("grp", "hid"), None, None),
            P(("grp", "hid"), None),
        ),
        out_specs=P(("grp", "hid"), None),
        check_vma=False,
    )
```
